32 devices in a mesh: group: 2 (over y), col: 4 (over z), row: 2 (over x), section: 2 (over core).
Axes of the slice: x: 2, y: 2, z: 4, core: 2. Of those that a mesh axis runs over, the one named last changes fastest.
Arguments:
- tokens: bfloat16 [2, 256, 8192], P(None, ('group', 'col'), 'row'), parts along dimension 1, may hold values from -12 to 12, as said below
- norm_gain: float32 [2, 8192], P('section', 'row'), may hold values from 0.5 to 1.5
- w_gate: bfloat16 [2, 8192, 14336], P('section', 'row', 'col'), may hold values from -0.0625 to 0.0625
- w_up: bfloat16 [2, 8192, 14336], P('section', 'row', 'col'), may hold values from -0.0625 to 0.0625
- w_down: bfloat16 [2, 14336, 8192], P('section', 'col', 'row'), may hold values from -0.046875 to 0.046875
Outputs:
- block_out: bfloat16 [2, 2, 256, 8192], P('section', None, ('group', 'col'), 'row'), parts along dimension 2
The draws below stay inside these ranges and needn't reach their ends.
There are 2 independent parts, one for each index of `group`. The reference program is written for one: setup_inputs(seed, part) draws one part's arguments, and reference() takes and returns one part's arrays. A program takes and returns all parts, laid end to end along the dimension named above; an argument that names none is the same for every part. Nothing has to cross between parts.
Inputs may be any that keep to these rules, and one draw needn't show every extreme that they name: `tokens`: dense real activations.
All inputs are finite; a program needn't handle non-finite values.
Results may differ from the reference program's by a relative error of at most 0.024.
Values may be sent and summed in bfloat16 or wider, within the bound.
No kernel may reach another device: no remote copies, remote signals or barrier semaphores. Data moves between devices by JAX's collectives and lax.ppermute only.
A program may use at most 128 MiB of HBM per device.

```python
import jax
import jax.numpy as jnp
from jax import lax

D = 8192
FF = 14336
MB = 2
TOK = 128
LAYERS = 2
N_COL = 4
N_ROW = 2


def draw_tokens(key, part):
    first_key, second_key = jax.random.split(jax.random.fold_in(key, 11))
    position = jnp.arange(D, dtype=jnp.float32) / D
    columns = 0.4 * jnp.exp(jnp.log(3.0) * position)
    rows = 0.5 * jnp.exp(jnp.log(3.0) * jax.random.uniform(second_key, (MB, TOK, 1), jnp.float32))
    values = jnp.clip(jax.random.normal(first_key, (MB, TOK, D), jnp.float32), -6.0, 6.0)
    return (values * columns[None, None, :] * rows).astype(jnp.bfloat16)


def block_scale(rng, shape, cuts, smallest, top_value):
    level = 1.0
    for dim, shards_of in cuts:
        steps = jax.random.uniform(jax.random.fold_in(jax.random.fold_in(rng, 6), dim), (shards_of,), jnp.float32, smallest / len(cuts), top_value / len(cuts))
        level = level * jnp.repeat(jnp.exp(steps), shape[dim] // shards_of).reshape((-1,) + (1,) * (len(shape) - 1 - dim))
    return level


def bell_draw(key, shape, width, bound, cuts=(), kind=jnp.bfloat16):
    level = block_scale(key, shape, cuts, -0.22, 0.18) if cuts else 1.0
    drawn = jax.random.normal(key, shape, jnp.float32) * width * level
    return jnp.minimum(jnp.maximum(drawn, -bound), bound).astype(kind)


def setup_inputs(seed: int = 0, part: int = 0) -> dict:
    keys = jax.random.split(jax.random.key(seed), 6)
    part_splits = jax.random.split(jax.random.fold_in(keys[5], part), 6)
    return {
        "tokens": draw_tokens(jax.random.fold_in(jax.random.fold_in(keys[5], part), 71), part),
        "norm_gain": jnp.clip(0.5 + 1.0 * jax.random.uniform(keys[1], (LAYERS, D), jnp.float32) ** block_scale(keys[1], (LAYERS, D), ((0, 2), (1, 2)), -0.2, 0.2), 0.5, 1.5),
        "w_gate": bell_draw(keys[2], (LAYERS, D, FF), D ** -0.5, 0.0625, ((0, 2), (1, 2), (2, 4))),
        "w_up": bell_draw(keys[3], (LAYERS, D, FF), D ** -0.5, 0.0625, ((0, 2), (1, 2), (2, 4))),
        "w_down": bell_draw(keys[4], (LAYERS, FF, D), FF ** -0.5, 0.046875, ((0, 2), (1, 4), (2, 2))),
    }


EPS = 1e-05

def rounded(value):
    return lax.optimization_barrier(value.astype(jnp.bfloat16)).astype(jnp.float32)

def one_block(h_in, gain, w_gate, w_up, w_down):
    wide = h_in.astype(jnp.float32)
    mean_sq = lax.optimization_barrier(jnp.mean(wide * wide, axis=1, keepdims=True))
    normed = (wide * lax.rsqrt(mean_sq + EPS) * gain[None, :]).astype(jnp.bfloat16)
    row_block = D // N_ROW
    gate = jnp.zeros((h_in.shape[0], FF), jnp.float32)
    up = jnp.zeros((h_in.shape[0], FF), jnp.float32)
    for index in range(N_ROW):
        piece = normed[:, index * row_block:(index + 1) * row_block]
        gate = gate + rounded(jnp.dot(piece, w_gate[index * row_block:(index + 1) * row_block], preferred_element_type=jnp.float32))
        up = up + rounded(jnp.dot(piece, w_up[index * row_block:(index + 1) * row_block], preferred_element_type=jnp.float32))
    hidden = (jax.nn.silu(gate) * up).astype(jnp.bfloat16)
    col_block = FF // N_COL
    ffn = jnp.zeros((h_in.shape[0], D), jnp.float32)
    for index in range(N_COL):
        piece = hidden[:, index * col_block:(index + 1) * col_block]
        ffn = ffn + rounded(jnp.dot(piece, w_down[index * col_block:(index + 1) * col_block], preferred_element_type=jnp.float32))
    return (wide + ffn).astype(jnp.bfloat16)

def reference(tokens, norm_gain, w_gate, w_up, w_down):
    layers_out = []
    current = [tokens[m] for m in range(MB)]
    for layer in range(LAYERS):
        current = [one_block(current[m], norm_gain[layer], w_gate[layer], w_up[layer], w_down[layer]) for m in range(MB)]
        layers_out.append(jnp.stack(current, axis=0))
    return jnp.stack(layers_out, axis=0)
```

```python
import jax
import jax.numpy as jnp
from jax import lax
from jax.experimental import pallas as pl
from jax.experimental.pallas import tpu as pltpu
from jax.sharding import PartitionSpec as P

EPS = 1e-05
MIB = 1 << 20
LANES = 128
BUFFERS = 3
VMEM_MIB = 12
PIECES = 8
AXES = ("group", "col", "row", "section")

f32 = jnp.float32
bf16 = jnp.bfloat16


def tile_of(width):
    for tile in (512, 256, 128):
        if width % tile == 0:
            return tile
    return width


def in_vmem(value):
    return pltpu.with_memory_space_constraint(value, pltpu.VMEM)


def in_hbm(value):
    return pltpu.with_memory_space_constraint(value, pltpu.HBM)


VMEM_SPEC = pl.BlockSpec(memory_space=pltpu.VMEM)
HBM_SPEC = pl.BlockSpec(memory_space=pltpu.HBM)
ANY_SPEC = pl.BlockSpec(memory_space=pl.ANY)


class Routes:
    def __init__(self, sizes):
        self.sizes = sizes

    def index(self, place):
        index = 0
        for axis in AXES:
            index = index * self.sizes[axis] + place[axis]
        return index

    def places(self):
        for g in range(self.sizes["group"]):
            for c in range(self.sizes["col"]):
                for r in range(self.sizes["row"]):
                    for s in range(self.sizes["section"]):
                        yield dict(group=g, col=c, row=r, section=s)

    def shifted(self, place, axis, steps):
        return dict(place, **{axis: (place[axis] + steps) % self.sizes[axis]})

    def within(self, section, axis, steps):
        pairs = []
        for place in self.places():
            if place["section"] == section:
                target = self.shifted(place, axis, steps)
            else:
                target = self.shifted(place, "group", 1)
            pairs.append((self.index(place), self.index(target)))
        return pairs

    def onward(self, section, steps):
        pairs = []
        for place in self.places():
            if place["section"] == section:
                target = dict(self.shifted(place, "col", steps), section=section + 1)
            elif place["section"] == section + 1:
                target = dict(place, section=section)
            else:
                target = self.shifted(place, "group", 1)
            pairs.append((self.index(place), self.index(target)))
        return pairs


def streamed(count, parts, copy, body):
    def start(q):
        tile, part = (q // parts, q % parts) if isinstance(q, int) else (lax.div(q, parts), lax.rem(q, parts))
        copy(tile, part, q % BUFFERS if isinstance(q, int) else lax.rem(q, BUFFERS)).start()

    for q in range(min(BUFFERS, count * parts)):
        start(q)

    def step(i, carry):
        def use(part, f):
            q = i * parts + part
            slot = lax.rem(q, BUFFERS)
            copy(i, part, slot).wait()
            value = f(slot)

            @pl.when(q + BUFFERS < count * parts)
            def _():
                start(q + BUFFERS)

            return value

        body(i, use)
        return carry

    return lambda: lax.fori_loop(0, count, step, 0)


class Kernels:
    def __init__(self, n_row, n_col, w_gate, w_up, w_down):
        self.n_row, self.n_col = n_row, n_col
        self.w_up, self.w_down = w_up, w_down
        self.kept = []
        self.before = []
        self.depth, self.width = w_gate.shape[1:]
        self.half = self.depth // 2
        self.load(w_gate)

    def call(self, kernel, operands, specs, out_shape, scratch, vmem, flops, moved, name):
        extras = [in_vmem(v) for v in self.kept] + self.before
        n_kept, n = len(self.kept), len(extras)

        def wrapped(*refs):
            kernel(refs[:n_kept], *refs[n:])

        outs = pl.pallas_call(
            wrapped,
            out_shape=out_shape,
            in_specs=[VMEM_SPEC] * n_kept + [ANY_SPEC] * (n - n_kept) + specs,
            out_specs=[VMEM_SPEC] * len(out_shape),
            scratch_shapes=scratch,
            compiler_params=pltpu.CompilerParams(vmem_limit_bytes=vmem * MIB),
            cost_estimate=pl.CostEstimate(flops=flops, bytes_accessed=moved, transcendentals=0),
            name=name,
        )(*extras, *operands)
        self.before = [outs[-1]]
        return outs

    def load(self, w_gate):
        rows = self.depth // PIECES

        def kernel(_, gate_ref, *refs):
            outs, sem = refs[:-1], refs[-1]
            copies = [
                pltpu.make_async_copy(gate_ref.at[0, pl.ds(i * rows, rows)], out, sem.at[i])
                for i, out in enumerate(outs)
            ]
            for copy in copies:
                copy.start()
            for copy in copies:
                copy.wait()

        self.kept = self.call(
            kernel,
            [in_hbm(w_gate)],
            [HBM_SPEC],
            [pltpu.VMEM((rows, self.width), bf16)] * PIECES,
            [pltpu.SemaphoreType.DMA((PIECES,))],
            1,
            0,
            2 * self.depth * self.width,
            "load",
        )
        self.before = []

    def gate_up(self, blocks, scaled_in, gain, start, size, tile):
        n_row, depth, half = self.n_row, self.depth, self.half
        opens = scaled_in is None
        n = len(blocks) if opens else 1
        rows = sum(b.shape[0] for b in blocks) if opens else scaled_in.shape[0]
        keep_rows = rows // n_row
        extra = LANES if opens else 0
        piece = depth // PIECES

        def scale_rows(block_refs, gain_ref, scaled, ssq):
            row = lax.axis_index("row")
            tok = block_refs[0].shape[0]
            per_piece = n // n_row
            for d, block in enumerate(block_refs):
                away = lax.rem(d // per_piece - row + n_row, n_row)
                place = pl.ds(pl.multiple_of((away * per_piece + d % per_piece) * tok, tok), tok)
                wide = block[...].astype(f32)
                scaled[place, :] = (wide * gain_ref[...]).astype(bf16)
                total = jnp.sum(wide * wide, axis=1, keepdims=True)
                ssq[place, :] = jnp.broadcast_to(total, (tok, LANES))

        def kernel(kept, *refs):
            sources, gain_ref, up_w, refs = refs[:n], refs[n], refs[n + 1], refs[n + 2 :]
            refs, (buf, sem) = refs[:-2], refs[-2:]
            keep, sends = refs[0], refs[1:n_row]

            def copy(i, part, slot):
                columns = pl.ds(pl.multiple_of(start + i * tile, LANES), tile)
                return pltpu.make_async_copy(
                    up_w.at[0, pl.ds(part * half, half), columns], buf.at[slot], sem.at[slot]
                )

            def body(i, use):
                offset = pl.multiple_of(i * tile, tile)
                columns = pl.ds(pl.multiple_of(start + offset, LANES), tile)

                def product(first, weights):
                    return jnp.dot(
                        scaled[:, first : first + weights.shape[0]], weights, preferred_element_type=f32
                    )

                gate = product(0, kept[0][:, columns])
                for p in range(1, PIECES):
                    gate = gate + product(p * piece, kept[p][:, columns])
                up = use(0, lambda slot: product(0, buf[slot]))
                up = up + use(1, lambda slot: product(half, buf[slot]))
                for part, base in ((gate, 0), (up, size)):
                    part = part.astype(bf16)
                    place = pl.ds(pl.multiple_of(base + offset, tile), tile)
                    keep[:, place] = part[:keep_rows]
                    for e, send in enumerate(sends, 1):
                        send[:, place] = part[e * keep_rows : (e + 1) * keep_rows]

            run = streamed(size // tile, 2, copy, body)
            if opens:
                scaled, ssq = refs[n_row:]
                scale_rows(sources, gain_ref, scaled, ssq)
                lane = lax.broadcasted_iota(jnp.int32, (keep_rows, LANES), 1)
                for e, send in enumerate(sends, 1):
                    total = ssq[pl.ds(e * keep_rows, keep_rows), :]
                    high = total.astype(bf16).astype(f32)
                    send[:, pl.ds(2 * size, LANES)] = jnp.where(
                        lane < LANES // 2, high, total - high
                    ).astype(bf16)
            else:
                scaled = sources[0]
            run()

        out_shape = [pltpu.VMEM((keep_rows, 2 * size), bf16)]
        out_shape += [jax.ShapeDtypeStruct((keep_rows, 2 * size + extra), bf16)] * (n_row - 1)
        if opens:
            out_shape += [pltpu.VMEM((rows, depth), bf16), pltpu.VMEM((rows, LANES), f32)]
        sources = list(blocks) if opens else [in_vmem(scaled_in)]
        return self.call(
            kernel,
            sources + [gain, in_hbm(self.w_up)],
            [VMEM_SPEC] * (n + 1) + [HBM_SPEC],
            out_shape,
            [
                pltpu.VMEM((BUFFERS, half, tile), bf16),
                pltpu.SemaphoreType.DMA((BUFFERS,)),
            ],
            VMEM_MIB,
            4 * rows * depth * size,
            2 * depth * size,
            "gate_up",
        )

    def hidden(self, keep, received, own, opens):
        rows, size = keep.shape[0], keep.shape[1] // 2
        n = len(received)
        features = self.depth * self.n_row

        def kernel(_, keep_ref, *refs):
            arrived, own_ref, out, scale_out = refs[:n], refs[n], refs[n + 1], refs[n + 2]
            if opens:
                total = own_ref[pl.ds(0, rows), 0:1]
                for ref in arrived:
                    tail = ref[:, pl.ds(2 * size, LANES)].astype(f32)
                    total = total + (tail[:, 0:1] + tail[:, LANES // 2 : LANES // 2 + 1])
                scale = lax.rsqrt(total / features + EPS)
            else:
                scale = own_ref[:, 0:1]
            scale_out[...] = jnp.broadcast_to(scale, (rows, LANES))
            gate = keep_ref[:, pl.ds(0, size)].astype(f32)
            up = keep_ref[:, pl.ds(size, size)].astype(f32)
            for ref in arrived:
                gate = gate + ref[:, pl.ds(0, size)].astype(f32)
                up = up + ref[:, pl.ds(size, size)].astype(f32)
            gate = gate * scale
            out[...] = (gate / (1.0 + jnp.exp(-gate)) * (up * scale)).astype(bf16)

        return self.call(
            kernel,
            [in_vmem(keep), *received, in_vmem(own)],
            [VMEM_SPEC] * (n + 2),
            [jax.ShapeDtypeStruct((rows, size), bf16), pltpu.VMEM((rows, LANES), f32)],
            [],
            4,
            0,
            2 * MIB,
            "hidden",
        )

    def down(self, pieces, start, size, acc):
        n_row, n_col = self.n_row, self.n_col
        keep_rows = pieces[0].shape[0]
        rows = keep_rows * n_row
        tok = rows // n_col
        columns = self.w_down.shape[2]
        tile = tile_of(columns)
        last = acc is not None

        def kernel(_, *refs):
            piece_refs, w_ref, refs = refs[:n_row], refs[n_row], refs[n_row + 1 :]
            if last:
                acc_ref, refs = refs[0], refs[1:]
            outs, (held, buf, sem) = refs[:-3], refs[-3:]
            row = lax.axis_index("row")

            def copy(i, _, slot):
                place = pl.ds(pl.multiple_of(i * tile, tile), tile)
                return pltpu.make_async_copy(
                    w_ref.at[0, pl.ds(start, size), place], buf.at[slot], sem.at[slot]
                )

            def body(i, use):
                place = pl.ds(pl.multiple_of(i * tile, tile), tile)
                part = use(0, lambda slot: jnp.dot(held[...], buf[slot], preferred_element_type=f32))
                if last:
                    part = (part + acc_ref[:, place]).astype(bf16)
                    for d, out in enumerate(outs):
                        out[:, place] = part[d * tok : (d + 1) * tok]
                else:
                    outs[0][:, place] = part

            run = streamed(columns // tile, 1, copy, body)
            for e, piece in enumerate(piece_refs):
                place = pl.multiple_of(lax.rem(row - e + n_row, n_row) * keep_rows, keep_rows)
                held[pl.ds(place, keep_rows), :] = piece[...]
            run()

        if last:
            out_shape = [jax.ShapeDtypeStruct((tok, columns), bf16)] * n_col
        else:
            out_shape = [pltpu.VMEM((rows, columns), f32)]
        return self.call(
            kernel,
            list(pieces) + [in_hbm(self.w_down)] + ([in_vmem(acc)] if last else []),
            [VMEM_SPEC] * n_row + [HBM_SPEC] + [VMEM_SPEC] * last,
            out_shape,
            [
                pltpu.VMEM((rows, size), bf16),
                pltpu.VMEM((BUFFERS, size, tile), bf16),
                pltpu.SemaphoreType.DMA((BUFFERS,)),
            ],
            VMEM_MIB,
            2 * rows * size * columns,
            2 * size * columns,
            "down",
        )


def solution(mesh):
    sizes = dict(mesh.shape)
    routes = Routes(sizes)
    n_col, n_row, n_section = sizes["col"], sizes["row"], sizes["section"]

    def move(value, pairs):
        return lax.ppermute(value, AXES, pairs)

    def on_device(tokens, norm_gain, w_gate, w_up, w_down):
        section_index = lax.axis_index("section")
        micro, tok, depth = tokens.shape
        width = w_gate.shape[2]
        tile = tile_of(width)
        cut = (width // tile + 1) // 2 * tile
        chunks = ((0, cut), (cut, width - cut))
        k = Kernels(n_row, n_col, w_gate, w_up, w_down)

        def gathered(section, block):
            if section == 0:
                return [block] + [move(block, routes.within(0, "col", d)) for d in range(1, n_col)]
            return [move(block, routes.onward(section - 1, d)) for d in range(n_col)]

        def exchanged(section, sends):
            return [move(v, routes.within(section, "row", e)) for e, v in enumerate(sends, 1)]

        class Job:
            def __init__(self, section, block):
                self.section = section
                self.blocks = gathered(section, block)

            def gate_up(self, c):
                if c == 0:
                    self.keep0, *sends, self.scaled, self.ssq = k.gate_up(
                        self.blocks, None, norm_gain, *chunks[0], tile
                    )
                    self.in0 = exchanged(self.section, sends)
                else:
                    self.keep1, *sends = k.gate_up(None, self.scaled, norm_gain, *chunks[1], tile)
                    self.in1 = exchanged(self.section, sends)

            def hidden(self, c):
                if c == 0:
                    out, self.scale = k.hidden(self.keep0, self.in0, self.ssq, True)
                    self.pieces0 = [out] + exchanged(self.section, [out] * (n_row - 1))
                else:
                    out, _ = k.hidden(self.keep1, self.in1, self.scale, False)
                    self.pieces1 = [out] + exchanged(self.section, [out] * (n_row - 1))

            def down(self, c):
                if c == 0:
                    (self.acc,) = k.down(self.pieces0, *chunks[0], None)
                else:
                    parts = k.down(self.pieces1, *chunks[1], self.acc)
                    arrived = [
                        move(parts[d], routes.within(self.section, "col", -d)) for d in range(1, n_col)
                    ]
                    total = parts[0].astype(f32)
                    for value in arrived:
                        total = total + value.astype(f32)
                    self.result = (self.blocks[0].astype(f32) + total).astype(bf16)

        current = [tokens[m] for m in range(micro)]
        outs = []
        for section in range(n_section):
            jobs = []
            for m in range(micro):
                block = current[m]
                if m and section == 0:
                    block, _ = lax.optimization_barrier((block, jobs[m - 1].blocks))
                jobs.append(Job(section, block))
            steps = ORDER if micro == 2 else [(j, w, c) for j in range(micro) for w in "ghd" for c in (0, 1)]
            uses = [step for step in steps if step[1] == "g"]
            for step in steps:
                j, what, c = step
                getattr(jobs[j], dict(g="gate_up", h="hidden", d="down")[what])(c)
                if section == n_section - 1 and step == uses[-1]:
                    k.kept = []
            current = [job.result for job in jobs]
            outs.append(jnp.stack(current, axis=0))
        out = outs[0]
        for section in range(1, n_section):
            out = jnp.where(section_index == section, outs[section], out)
        return out[None]

    placed = (
        P(None, ("group", "col"), "row"),
        P("section", "row"),
        P("section", "row", "col"),
        P("section", "row", "col"),
        P("section", "col", "row"),
    )
    return jax.shard_map(
        on_device,
        mesh=mesh,
        in_specs=placed,
        out_specs=P("section", None, ("group", "col"), "row"),
        check_vma=False,
    )


ORDER = [
    (0, "g", 0), (0, "g", 1), (1, "g", 0), (0, "h", 0), (0, "h", 1), (1, "g", 1),
    (0, "d", 0), (1, "h", 0), (0, "d", 1), (1, "h", 1), (1, "d", 0), (1, "d", 1),
]
```

```python
import jax
import jax.numpy as jnp
from jax import lax
from jax.experimental import pallas as pl
from jax.experimental.pallas import tpu as pltpu
from jax.sharding import PartitionSpec as P

EPS = 1e-05
MIB = 1 << 20
LANES = 128
BUFFERS = 3
VMEM_MIB = 12
PIECES = 8
PARTS = 2
WIDEST = 2048
AXES = ("group", "col", "row", "section")

f32 = jnp.float32
bf16 = jnp.bfloat16


def tile_of(width):
    for tile in (512, 256, 128):
        if width % tile == 0:
            return tile
    return width


def in_vmem(value):
    return pltpu.with_memory_space_constraint(value, pltpu.VMEM)


def in_hbm(value):
    return pltpu.with_memory_space_constraint(value, pltpu.HBM)


VMEM_SPEC = pl.BlockSpec(memory_space=pltpu.VMEM)
HBM_SPEC = pl.BlockSpec(memory_space=pltpu.HBM)
ANY_SPEC = pl.BlockSpec(memory_space=pl.ANY)


class Routes:
    def __init__(self, sizes):
        self.sizes = sizes

    def index(self, place):
        index = 0
        for axis in AXES:
            index = index * self.sizes[axis] + place[axis]
        return index

    def places(self):
        for g in range(self.sizes["group"]):
            for c in range(self.sizes["col"]):
                for r in range(self.sizes["row"]):
                    for s in range(self.sizes["section"]):
                        yield dict(group=g, col=c, row=r, section=s)

    def shifted(self, place, axis, steps):
        return dict(place, **{axis: (place[axis] + steps) % self.sizes[axis]})

    def within(self, section, axis, steps):
        pairs = []
        for place in self.places():
            if place["section"] == section:
                target = self.shifted(place, axis, steps)
            else:
                target = self.shifted(place, "group", 1)
            pairs.append((self.index(place), self.index(target)))
        return pairs

    def onward(self, section, steps):
        pairs = []
        for place in self.places():
            if place["section"] == section:
                target = dict(self.shifted(place, "col", steps), section=section + 1)
            elif place["section"] == section + 1:
                target = dict(place, section=section)
            else:
                target = self.shifted(place, "group", 1)
            pairs.append((self.index(place), self.index(target)))
        return pairs


def streamed(count, parts, copy, body):
    def start(q):
        tile, part = (q // parts, q % parts) if isinstance(q, int) else (lax.div(q, parts), lax.rem(q, parts))
        copy(tile, part, q % BUFFERS if isinstance(q, int) else lax.rem(q, BUFFERS)).start()

    for q in range(min(BUFFERS, count * parts)):
        start(q)

    def step(i, carry):
        def use(part, f):
            q = i * parts + part
            slot = lax.rem(q, BUFFERS)
            copy(i, part, slot).wait()
            value = f(slot)

            @pl.when(q + BUFFERS < count * parts)
            def _():
                start(q + BUFFERS)

            return value

        body(i, use)
        return carry

    return lambda: lax.fori_loop(0, count, step, 0)


class Kernels:
    def __init__(self, n_row, n_col, w_gate, w_up, w_down):
        self.n_row, self.n_col = n_row, n_col
        self.w_up, self.w_down = w_up, w_down
        self.kept = []
        self.before = []
        self.depth, self.width = w_gate.shape[1:]
        self.half = self.depth // PARTS
        self.load(w_gate)

    def call(self, section, kernel, operands, specs, out_shape, scratch, vmem, flops, moved, name):
        extras = [in_vmem(v) for v in self.kept] + self.before
        n_kept, n = len(self.kept), len(extras)

        def wrapped(*refs):
            if section is None:
                kernel(refs[:n_kept], *refs[n:])
            else:

                @pl.when(lax.axis_index("section") == section)
                def _():
                    kernel(refs[:n_kept], *refs[n:])

        outs = pl.pallas_call(
            wrapped,
            out_shape=out_shape,
            in_specs=[VMEM_SPEC] * n_kept + [ANY_SPEC] * (n - n_kept) + specs,
            out_specs=[VMEM_SPEC] * len(out_shape),
            scratch_shapes=scratch,
            compiler_params=pltpu.CompilerParams(vmem_limit_bytes=vmem * MIB),
            cost_estimate=pl.CostEstimate(flops=flops, bytes_accessed=moved, transcendentals=0),
            name=name,
        )(*extras, *operands)
        self.before = [outs[-1]]
        return outs

    def load(self, w_gate):
        rows = self.depth // PIECES
        n = PIECES

        def kernel(_, gate_ref, *refs):
            outs, sem = refs[:-1], refs[-1]
            copies = []
            for i, out in enumerate(outs):
                copies.append(pltpu.make_async_copy(gate_ref.at[0, pl.ds(i * rows, rows)], out, sem.at[i]))
            for copy in copies:
                copy.start()
            for copy in copies:
                copy.wait()

        self.kept = self.call(
            None,
            kernel,
            [in_hbm(w_gate)],
            [HBM_SPEC],
            [pltpu.VMEM((rows, self.width), bf16)] * n,
            [pltpu.SemaphoreType.DMA((n,))],
            1,
            0,
            2 * n * rows * self.width,
            "load",
        )
        self.before = []

    def gate_up(self, section, blocks, scaled_in, gain, start, size, tile):
        depth, half = self.depth, self.half
        opens = scaled_in is None
        n = len(blocks) if opens else 1
        rows = sum(b.shape[0] for b in blocks) if opens else scaled_in.shape[0]
        extra = LANES if opens else 0
        piece = depth // PIECES

        def scale_rows(block_refs, gain_ref, scaled, out):
            tok = block_refs[0].shape[0]
            lane = lax.broadcasted_iota(jnp.int32, (tok, LANES), 1)
            for d, block in enumerate(block_refs):
                place = slice(d * tok, (d + 1) * tok)
                total = jnp.zeros((tok, LANES), f32)
                for first in range(0, depth, tile):
                    wide = block[:, first : first + tile].astype(f32)
                    scaled[place, first : first + tile] = (
                        wide * gain_ref[:, first : first + tile]
                    ).astype(bf16)
                    wide = wide * wide
                    for lane_first in range(0, tile, LANES):
                        total = total + wide[:, lane_first : lane_first + LANES]
                total = jnp.broadcast_to(jnp.sum(total, axis=1, keepdims=True), (tok, LANES))
                high = total.astype(bf16).astype(f32)
                out[place, pl.ds(2 * size, LANES)] = jnp.where(
                    lane < LANES // 2, high, total - high
                ).astype(bf16)

        def kernel(kept, *refs):
            sources, gain_ref, up_w, refs = refs[:n], refs[n], refs[n + 1], refs[n + 2 :]
            out, buf, sem = refs[0], refs[-2], refs[-1]

            def copy(i, part, slot):
                columns = pl.ds(pl.multiple_of(start + i * tile, LANES), tile)
                return pltpu.make_async_copy(
                    up_w.at[0, pl.ds(part * half, half), columns], buf.at[slot], sem.at[slot]
                )

            def body(i, use):
                offset = pl.multiple_of(i * tile, tile)
                columns = pl.ds(pl.multiple_of(start + offset, LANES), tile)

                def product(first, weights):
                    return jnp.dot(
                        scaled[:, first : first + weights.shape[0]], weights, preferred_element_type=f32
                    )

                gate = product(0, kept[0][:, columns])
                for p in range(1, PIECES):
                    gate = gate + product(p * piece, kept[p][:, columns])
                out[:, pl.ds(offset, tile)] = gate.astype(bf16)
                up = use(0, lambda slot: product(0, buf[slot]))
                for part in range(1, PARTS):
                    up = up + use(part, lambda slot: product(part * half, buf[slot]))
                out[:, pl.ds(pl.multiple_of(size + offset, tile), tile)] = up.astype(bf16)

            run = streamed(size // tile, PARTS, copy, body)
            scaled = sources[0]
            if opens:
                scaled = refs[1]
                scale_rows(sources, gain_ref, scaled, out)
            run()

        out_shape = [pltpu.VMEM((rows, 2 * size + extra), bf16)]
        if opens:
            out_shape += [pltpu.VMEM((rows, depth), bf16)]
        sources = [in_vmem(v) for v in blocks] if opens else [in_vmem(scaled_in)]
        return self.call(
            section,
            kernel,
            sources + [gain, in_hbm(self.w_up)],
            [VMEM_SPEC] * (n + 1) + [HBM_SPEC],
            out_shape,
            [
                pltpu.VMEM((BUFFERS, half, tile), bf16),
                pltpu.SemaphoreType.DMA((BUFFERS,)),
            ],
            VMEM_MIB,
            4 * rows * depth * size,
            2 * depth * size,
            "gate_up",
        )

    def down(self, section, sums, chunks, scale_in, acc):
        n_row, n_col = self.n_row, self.n_col
        start, size = chunks[0][0], sum(chunk[1] for chunk in chunks)
        rows = sums[0][0].shape[0]
        tok = rows // n_col
        columns = self.w_down.shape[2]
        tile = tile_of(columns)
        opens, last = start == 0, start + size == self.width
        parts = -(-size // WIDEST)
        deep = size // parts
        features = self.depth * n_row
        flat = [in_vmem(v) for group in sums for v in group]
        n = len(flat)

        def kernel(_, *refs):
            sum_refs, w_ref, refs = refs[:n], refs[n], refs[n + 1 :]
            if not opens:
                scale_ref, acc_ref, refs = refs[0], refs[1], refs[2:]
            outs, (held, buf, sem) = refs[:-3], refs[-3:]

            def copy(i, part, slot):
                place = pl.ds(pl.multiple_of(i * tile, tile), tile)
                return pltpu.make_async_copy(
                    w_ref.at[0, pl.ds(start + part * deep, deep), place], buf.at[slot], sem.at[slot]
                )

            def body(i, use):
                place = pl.ds(pl.multiple_of(i * tile, tile), tile)
                total = None if opens else acc_ref[:, place]
                for p in range(parts):
                    left = held[:, p * deep : (p + 1) * deep]
                    part = use(p, lambda slot: jnp.dot(left, buf[slot], preferred_element_type=f32))
                    total = part if total is None else total + part
                if last:
                    total = total.astype(bf16)
                    for d, out in enumerate(outs):
                        out[:, place] = total[d * tok : (d + 1) * tok]
                else:
                    outs[0][:, place] = total

            run = streamed(columns // tile, parts, copy, body)
            for first in range(0, rows, tok):
                place = slice(first, first + tok)
                for c, (begin, width) in enumerate(chunks):
                    refs_here = sum_refs[c * n_row : (c + 1) * n_row]

                    def whole(columns):
                        total = refs_here[0][place, columns].astype(f32)
                        for ref in refs_here[1:]:
                            total = total + ref[place, columns].astype(f32)
                        return total

                    if c == 0 and opens:
                        squares = whole(pl.ds(2 * width, LANES))
                        squares = squares[:, 0:1] + squares[:, LANES // 2 : LANES // 2 + 1]
                        scale = lax.rsqrt(squares / features + EPS)
                    elif c == 0:
                        scale = scale_ref[place, 0:1]
                    step = tile_of(width)
                    for at in range(0, width, step):
                        gate = whole(pl.ds(at, step)) * scale
                        up = whole(pl.ds(width + at, step)) * scale
                        held[place, begin - start + at : begin - start + at + step] = (
                            gate / (1.0 + jnp.exp(-gate)) * up
                        ).astype(bf16)
                if not last:
                    outs[1][place, :] = jnp.broadcast_to(scale, (tok, LANES))
            run()

        if last:
            out_shape = [pltpu.VMEM((tok, columns), bf16)] * n_col
        else:
            out_shape = [pltpu.VMEM((rows, columns), f32), pltpu.VMEM((rows, LANES), f32)]
        extras = [] if opens else [in_vmem(scale_in), in_vmem(acc)]
        return self.call(
            section,
            kernel,
            flat + [in_hbm(self.w_down)] + extras,
            [VMEM_SPEC] * n + [HBM_SPEC] + [VMEM_SPEC] * len(extras),
            out_shape,
            [
                pltpu.VMEM((rows, size), bf16),
                pltpu.VMEM((BUFFERS, deep, tile), bf16),
                pltpu.SemaphoreType.DMA((BUFFERS,)),
            ],
            VMEM_MIB,
            2 * rows * size * columns,
            2 * size * columns,
            "down",
        )


def solution(mesh):
    sizes = dict(mesh.shape)
    routes = Routes(sizes)
    n_col, n_row, n_section = sizes["col"], sizes["row"], sizes["section"]

    def move(value, pairs):
        return lax.ppermute(value, AXES, pairs)

    def on_device(tokens, norm_gain, w_gate, w_up, w_down):
        section_index = lax.axis_index("section")
        micro, tok, depth = tokens.shape
        width = w_gate.shape[2]
        tile = tile_of(width)
        k = Kernels(n_row, n_col, w_gate, w_up, w_down)

        def gathered(section, block):
            if section:
                return [move(block, routes.onward(section - 1, d)) for d in range(n_col)]
            return [block] + [move(block, routes.within(section, "col", d)) for d in range(1, n_col)]

        def exchanged(section, value):
            return [value] + [move(value, routes.within(section, "row", e)) for e in range(1, n_row)]

        class Job:
            def __init__(self, section, block, chunks):
                self.section, self.chunks = section, chunks
                self.blocks = gathered(section, block)
                self.scaled = self.scale = self.acc = None
                self.sums = []

            def gate_up(self, c):
                outs = k.gate_up(self.section, self.blocks, self.scaled, norm_gain, *self.chunks[c], tile)
                if c == 0:
                    self.scaled = outs[1]
                self.sums.append(exchanged(self.section, outs[0]))

            def down(self, first, last):
                outs = k.down(
                    self.section, self.sums[first:last], self.chunks[first:last], self.scale, self.acc
                )
                if last < len(self.chunks):
                    self.acc, self.scale = outs
                    return
                arrived = [
                    move(outs[d], routes.within(self.section, "col", -d)) for d in range(1, n_col)
                ]
                total = outs[0].astype(f32)
                for value in arrived:
                    total = total + value.astype(f32)
                self.result = (self.blocks[0].astype(f32) + total).astype(bf16)

        jobs = {}
        steps = FLAT if (n_section, micro) == (2, 2) else in_turn(n_section, micro)
        for at, (what, section, m, *c) in enumerate(steps):
            if what == "n":
                block = jobs[section - 1, m].result if section else tokens[m]
                if jobs:
                    block, _ = lax.optimization_barrier((block, k.before[0]))
                jobs[section, m] = Job(section, block, chunked(width, tile, *c))
            elif what == "g":
                jobs[section, m].gate_up(*c)
                if not any(step[0] == "g" for step in steps[at + 1 :]):
                    k.kept = []
            else:
                jobs[section, m].down(*c)
        outs = [
            jnp.stack([jobs[section, m].result for m in range(micro)], axis=0)
            for section in range(n_section)
        ]
        out = outs[0]
        for section in range(1, n_section):
            out = jnp.where(section_index == section, outs[section], out)
        return out[None]

    placed = (
        P(None, ("group", "col"), "row"),
        P("section", "row"),
        P("section", "row", "col"),
        P("section", "row", "col"),
        P("section", "col", "row"),
    )
    return jax.shard_map(
        on_device,
        mesh=mesh,
        in_specs=placed,
        out_specs=P("section", None, ("group", "col"), "row"),
        check_vma=False,
    )


def chunked(width, tile, count):
    tiles = width // tile
    chunks, start = [], 0
    for c in range(count):
        size = -(-(tiles - start // tile) // (count - c)) * tile
        chunks.append((start, size))
        start += size
    return chunks


def in_turn(n_section, micro):
    steps = []
    for section in range(n_section):
        for m in range(micro):
            steps += [("n", section, m, 2), ("g", section, m, 0), ("g", section, m, 1)]
            steps += [("d", section, m, 0, 2)]
    return steps


FLAT = [("n", 0, 0, 2), ("g", 0, 0, 0), ("n", 0, 1, 2), ("g", 0, 0, 1), ("g", 0, 1, 0), ("d", 0, 0, 0, 1), ("d", 0, 0, 1, 2), ("g", 0, 1, 1), ("d", 0, 1, 0, 1), ("n", 1, 0, 2), ("d", 0, 1, 1, 2),("g", 1, 0, 0), ("g", 1, 0, 1), ("n", 1, 1, 2), ("d", 1, 0, 0, 1), ("d", 1, 0, 1, 2), ("g", 1, 1, 0), ("g", 1, 1, 1), ("d", 1, 1, 0, 1), ("d", 1, 1, 1, 2),]
```

```python
import jax
import jax.numpy as jnp
from jax import lax
from jax.experimental import pallas as pl
from jax.experimental.pallas import tpu as pltpu
from jax.sharding import PartitionSpec as P

EPS = 1e-05
MIB = 1 << 20
LANES = 128
BUFFERS = 3
VMEM_MIB = 12
PIECES = 8
PARTS = 2
WIDEST = 2048
AXES = ("group", "col", "row", "section")

f32 = jnp.float32
bf16 = jnp.bfloat16


def tile_of(width):
    for tile in (512, 256, 128):
        if width % tile == 0:
            return tile
    return width


def in_vmem(value):
    return pltpu.with_memory_space_constraint(value, pltpu.VMEM)


def in_hbm(value):
    return pltpu.with_memory_space_constraint(value, pltpu.HBM)


VMEM_SPEC = pl.BlockSpec(memory_space=pltpu.VMEM)
HBM_SPEC = pl.BlockSpec(memory_space=pltpu.HBM)
ANY_SPEC = pl.BlockSpec(memory_space=pl.ANY)


class Routes:
    def __init__(self, sizes):
        self.sizes = sizes

    def index(self, place):
        index = 0
        for axis in AXES:
            index = index * self.sizes[axis] + place[axis]
        return index

    def places(self):
        for g in range(self.sizes["group"]):
            for c in range(self.sizes["col"]):
                for r in range(self.sizes["row"]):
                    for s in range(self.sizes["section"]):
                        yield dict(group=g, col=c, row=r, section=s)

    def shifted(self, place, axis, steps):
        return dict(place, **{axis: (place[axis] + steps) % self.sizes[axis]})

    def within(self, section, axis, steps):
        pairs = []
        for place in self.places():
            if place["section"] == section:
                target = self.shifted(place, axis, steps)
            else:
                target = self.shifted(place, "group", 1)
            pairs.append((self.index(place), self.index(target)))
        return pairs

    def onward(self, section, steps):
        pairs = []
        for place in self.places():
            if place["section"] == section:
                target = dict(self.shifted(place, "col", steps), section=section + 1)
            elif place["section"] == section + 1:
                target = dict(place, section=section)
            else:
                target = self.shifted(place, "group", 1)
            pairs.append((self.index(place), self.index(target)))
        return pairs


def streamed(count, parts, copy, body):
    def start(q):
        tile, part = (q // parts, q % parts) if isinstance(q, int) else (lax.div(q, parts), lax.rem(q, parts))
        copy(tile, part, q % BUFFERS if isinstance(q, int) else lax.rem(q, BUFFERS)).start()

    for q in range(min(BUFFERS, count * parts)):
        start(q)

    def step(i, carry):
        def use(part, f):
            q = i * parts + part
            slot = lax.rem(q, BUFFERS)
            copy(i, part, slot).wait()
            value = f(slot)

            @pl.when(q + BUFFERS < count * parts)
            def _():
                start(q + BUFFERS)

            return value

        body(i, use)
        return carry

    return lambda: lax.fori_loop(0, count, step, 0)


class Kernels:
    def __init__(self, n_row, n_col, w_gate, w_up, w_down):
        self.n_row, self.n_col = n_row, n_col
        self.w_up, self.w_down = w_up, w_down
        self.kept = []
        self.before = []
        self.share = 1
        self.depth, self.width = w_gate.shape[1:]
        self.half = self.depth // PARTS
        self.w_gate = w_gate

    def call(self, section, kernel, operands, specs, out_shape, scratch, vmem, flops, moved, name):
        extras = [in_vmem(v) for v in self.kept] + self.before
        n_kept, n = len(self.kept), len(extras)

        def wrapped(*refs):
            if section is None:
                kernel(refs[:n_kept], *refs[n:])
            else:

                @pl.when(lax.axis_index("section") == section)
                def _():
                    kernel(refs[:n_kept], *refs[n:])

        outs = pl.pallas_call(
            wrapped,
            out_shape=out_shape,
            in_specs=[VMEM_SPEC] * n_kept + [ANY_SPEC] * (n - n_kept) + specs,
            out_specs=[VMEM_SPEC] * len(out_shape),
            scratch_shapes=scratch,
            compiler_params=pltpu.CompilerParams(vmem_limit_bytes=vmem * MIB),
            cost_estimate=pl.CostEstimate(flops=flops // self.share, bytes_accessed=moved // self.share, transcendentals=0),
            name=name,
        )(*extras, *operands)
        self.before = [outs[-1]]
        return outs

    def load(self, section):
        self.kept = []
        rows = self.depth // PIECES
        n = PIECES

        def kernel(_, gate_ref, *refs):
            outs, sem = refs[:-1], refs[-1]
            copies = []
            for i, out in enumerate(outs):
                copies.append(pltpu.make_async_copy(gate_ref.at[0, pl.ds(i * rows, rows)], out, sem.at[i]))
            for copy in copies:
                copy.start()
            for copy in copies:
                copy.wait()

        self.kept = self.call(
            section,
            kernel,
            [in_hbm(self.w_gate)],
            [HBM_SPEC],
            [pltpu.VMEM((rows, self.width), bf16)] * n,
            [pltpu.SemaphoreType.DMA((n,))],
            1,
            0,
            2 * n * rows * self.width,
            "load",
        )

    def gate_up(self, section, blocks, scaled_in, gain, start, size, tile):
        depth, half = self.depth, self.half
        opens = scaled_in is None
        n = len(blocks) if opens else 1
        rows = sum(b.shape[0] for b in blocks) if opens else scaled_in.shape[0]
        extra = LANES if opens else 0
        piece = depth // PIECES

        def scale_rows(block_refs, gain_ref, scaled, out):
            tok = block_refs[0].shape[0]
            lane = lax.broadcasted_iota(jnp.int32, (tok, LANES), 1)
            for d, block in enumerate(block_refs):
                place = slice(d * tok, (d + 1) * tok)
                total = jnp.zeros((tok, LANES), f32)
                for first in range(0, depth, tile):
                    wide = block[:, first : first + tile].astype(f32)
                    scaled[place, first : first + tile] = (
                        wide * gain_ref[:, first : first + tile]
                    ).astype(bf16)
                    wide = wide * wide
                    for lane_first in range(0, tile, LANES):
                        total = total + wide[:, lane_first : lane_first + LANES]
                total = jnp.broadcast_to(jnp.sum(total, axis=1, keepdims=True), (tok, LANES))
                high = total.astype(bf16).astype(f32)
                out[place, pl.ds(2 * size, LANES)] = jnp.where(
                    lane < LANES // 2, high, total - high
                ).astype(bf16)

        def kernel(kept, *refs):
            sources, gain_ref, up_w, refs = refs[:n], refs[n], refs[n + 1], refs[n + 2 :]
            out, buf, sem = refs[0], refs[-2], refs[-1]

            def copy(i, part, slot):
                columns = pl.ds(pl.multiple_of(start + i * tile, LANES), tile)
                return pltpu.make_async_copy(
                    up_w.at[0, pl.ds(part * half, half), columns], buf.at[slot], sem.at[slot]
                )

            def body(i, use):
                offset = pl.multiple_of(i * tile, tile)
                columns = pl.ds(pl.multiple_of(start + offset, LANES), tile)

                def product(first, weights):
                    return jnp.dot(
                        scaled[:, first : first + weights.shape[0]], weights, preferred_element_type=f32
                    )

                gate = product(0, kept[0][:, columns])
                for p in range(1, PIECES):
                    gate = gate + product(p * piece, kept[p][:, columns])
                out[:, pl.ds(offset, tile)] = gate.astype(bf16)
                up = use(0, lambda slot: product(0, buf[slot]))
                for part in range(1, PARTS):
                    up = up + use(part, lambda slot: product(part * half, buf[slot]))
                out[:, pl.ds(pl.multiple_of(size + offset, tile), tile)] = up.astype(bf16)

            run = streamed(size // tile, PARTS, copy, body)
            scaled = sources[0]
            if opens:
                scaled = refs[1]
                scale_rows(sources, gain_ref, scaled, out)
            run()

        out_shape = [pltpu.VMEM((rows, 2 * size + extra), bf16)]
        if opens:
            out_shape += [pltpu.VMEM((rows, depth), bf16)]
        sources = [in_vmem(v) for v in blocks] if opens else [in_vmem(scaled_in)]
        return self.call(
            section,
            kernel,
            sources + [gain, in_hbm(self.w_up)],
            [VMEM_SPEC] * (n + 1) + [HBM_SPEC],
            out_shape,
            [
                pltpu.VMEM((BUFFERS, half, tile), bf16),
                pltpu.SemaphoreType.DMA((BUFFERS,)),
            ],
            VMEM_MIB,
            4 * rows * depth * size,
            2 * depth * size,
            "gate_up",
        )

    def down(self, section, sums, chunks, scale_in, acc):
        n_row, n_col = self.n_row, self.n_col
        start, size = chunks[0][0], sum(chunk[1] for chunk in chunks)
        rows = sums[0][0].shape[0]
        tok = rows // n_col
        columns = self.w_down.shape[2]
        tile = tile_of(columns)
        opens, last = start == 0, start + size == self.width
        parts = -(-size // WIDEST)
        deep = size // parts
        features = self.depth * n_row
        flat = [in_vmem(v) for group in sums for v in group]
        n = len(flat)

        def kernel(_, *refs):
            sum_refs, w_ref, refs = refs[:n], refs[n], refs[n + 1 :]
            if not opens:
                scale_ref, acc_ref, refs = refs[0], refs[1], refs[2:]
            outs, (held, buf, sem) = refs[:-3], refs[-3:]

            def copy(i, part, slot):
                place = pl.ds(pl.multiple_of(i * tile, tile), tile)
                return pltpu.make_async_copy(
                    w_ref.at[0, pl.ds(start + part * deep, deep), place], buf.at[slot], sem.at[slot]
                )

            def body(i, use):
                place = pl.ds(pl.multiple_of(i * tile, tile), tile)
                total = None if opens else acc_ref[:, place]
                for p in range(parts):
                    left = held[:, p * deep : (p + 1) * deep]
                    part = use(p, lambda slot: jnp.dot(left, buf[slot], preferred_element_type=f32))
                    total = part if total is None else total + part
                if last:
                    total = total.astype(bf16)
                    for d, out in enumerate(outs):
                        out[:, place] = total[d * tok : (d + 1) * tok]
                else:
                    outs[0][:, place] = total

            run = streamed(columns // tile, parts, copy, body)
            for first in range(0, rows, tok):
                place = slice(first, first + tok)
                for c, (begin, width) in enumerate(chunks):
                    refs_here = sum_refs[c * n_row : (c + 1) * n_row]

                    def whole(columns):
                        total = refs_here[0][place, columns].astype(f32)
                        for ref in refs_here[1:]:
                            total = total + ref[place, columns].astype(f32)
                        return total

                    if c == 0 and opens:
                        squares = whole(pl.ds(2 * width, LANES))
                        squares = squares[:, 0:1] + squares[:, LANES // 2 : LANES // 2 + 1]
                        scale = lax.rsqrt(squares / features + EPS)
                    elif c == 0:
                        scale = scale_ref[place, 0:1]
                    step = tile_of(width)
                    for at in range(0, width, step):
                        gate = whole(pl.ds(at, step)) * scale
                        up = whole(pl.ds(width + at, step)) * scale
                        held[place, begin - start + at : begin - start + at + step] = (
                            gate / (1.0 + jnp.exp(-gate)) * up
                        ).astype(bf16)
                if not last:
                    outs[1][place, :] = jnp.broadcast_to(scale, (tok, LANES))
            run()

        if last:
            out_shape = [pltpu.VMEM((tok, columns), bf16)] * n_col
        else:
            out_shape = [pltpu.VMEM((rows, columns), f32), pltpu.VMEM((rows, LANES), f32)]
        extras = [] if opens else [in_vmem(scale_in), in_vmem(acc)]
        return self.call(
            section,
            kernel,
            flat + [in_hbm(self.w_down)] + extras,
            [VMEM_SPEC] * n + [HBM_SPEC] + [VMEM_SPEC] * len(extras),
            out_shape,
            [
                pltpu.VMEM((rows, size), bf16),
                pltpu.VMEM((BUFFERS, deep, tile), bf16),
                pltpu.SemaphoreType.DMA((BUFFERS,)),
            ],
            VMEM_MIB,
            2 * rows * size * columns,
            2 * size * columns,
            "down",
        )


def solution(mesh):
    sizes = dict(mesh.shape)
    routes = Routes(sizes)
    n_col, n_row, n_section = sizes["col"], sizes["row"], sizes["section"]

    def move(value, pairs):
        return lax.ppermute(value, AXES, pairs)

    def on_device(tokens, norm_gain, w_gate, w_up, w_down):
        section_index = lax.axis_index("section")
        micro, tok, depth = tokens.shape
        width = w_gate.shape[2]
        tile = tile_of(width)
        k = Kernels(n_row, n_col, w_gate, w_up, w_down)

        def gathered(section, block):
            return [block] + [move(block, routes.within(section, "col", d)) for d in range(1, n_col)]

        def exchanged(section, value):
            return [value] + [move(value, routes.within(section, "row", e)) for e in range(1, n_row)]

        class Job:
            def __init__(self, section, block, chunks):
                self.section, self.chunks = section, chunks
                self.blocks = gathered(section, block)
                self.scaled = self.scale = self.acc = None
                self.sums = []

            def gate_up(self, c):
                outs = k.gate_up(self.section, self.blocks, self.scaled, norm_gain, *self.chunks[c], tile)
                if c == 0:
                    self.scaled = outs[1]
                self.sums.append(exchanged(self.section, outs[0]))

            def down(self, first, last):
                outs = k.down(
                    self.section, self.sums[first:last], self.chunks[first:last], self.scale, self.acc
                )
                if last < len(self.chunks):
                    self.acc, self.scale = outs
                    return
                block = self.blocks[0]
                if self.section + 1 < n_section:
                    arrived = [move(outs[d], routes.onward(self.section, -d)) for d in range(n_col)]
                    if self.section:
                        block = move(block, routes.onward(self.section, 0))
                else:
                    arrived = [outs[0]] + [
                        move(outs[d], routes.within(self.section, "col", -d)) for d in range(1, n_col)
                    ]
                total = block.astype(f32)
                for value in arrived:
                    total = total + value.astype(f32)
                self.result = total.astype(bf16)

        jobs = {}
        steps = FLAT if (n_section, micro) == (2, 2) else in_turn(n_section, micro)
        for at, (what, section, m, *c) in enumerate(steps):
            k.share = SHARES.get((what, section, m, *c), 1)
            if what == "n":
                block = jobs[section - 1, m].result if section else tokens[m]
                if k.before and jobs:
                    block, _ = lax.optimization_barrier((block, k.before[0]))
                jobs[section, m] = Job(section, block, chunked(width, tile, *c))
            elif what == "l":
                k.load(section)
            elif what == "g":
                jobs[section, m].gate_up(*c)
                later = [step[0] for step in steps[at + 1 :] if step[0] in "gl"]
                if later[:1] != ["g"]:
                    k.kept = []
            else:
                jobs[section, m].down(*c)
        outs = [
            jnp.stack([jobs[section, m].result for m in range(micro)], axis=0)
            for section in range(n_section)
        ]
        outs = [move(v, routes.onward(s, 0)) for s, v in enumerate(outs[:-1])] + outs[-1:]
        out = outs[0]
        for section in range(1, n_section):
            out = jnp.where(section_index == section, outs[section], out)
        return out[None]

    placed = (
        P(None, ("group", "col"), "row"),
        P("section", "row"),
        P("section", "row", "col"),
        P("section", "row", "col"),
        P("section", "col", "row"),
    )
    return jax.shard_map(
        on_device,
        mesh=mesh,
        in_specs=placed,
        out_specs=P("section", None, ("group", "col"), "row"),
        check_vma=False,
    )


def chunked(width, tile, count):
    tiles = width // tile
    chunks, start = [], 0
    for c in range(count):
        size = -(-(tiles - start // tile) // (count - c)) * tile
        chunks.append((start, size))
        start += size
    return chunks


def in_turn(n_section, micro):
    steps = []
    for section in range(n_section):
        steps += [("l", section, 0)]
        for m in range(micro):
            steps += [("n", section, m, 2), ("g", section, m, 0), ("g", section, m, 1)]
            steps += [("d", section, m, 0, 2)]
    return steps


SHARES = {("g", 1, 0, 0): 3, ("g", 1, 0, 1): 3, ("d", 1, 1, 0, 1): 10, ("d", 1, 1, 1, 2): 10}

FLAT = [
    ("l", None, 0),
    ("n", 0, 0, 2), ("g", 0, 0, 0), ("n", 0, 1, 2), ("g", 0, 0, 1), ("g", 0, 1, 0), ("d", 0, 0, 0, 1),
    ("d", 0, 0, 1, 2), ("g", 0, 1, 1), ("d", 0, 1, 0, 1), ("n", 1, 0, 2), ("d", 0, 1, 1, 2),
    ("g", 1, 0, 0), ("g", 1, 0, 1), ("n", 1, 1, 2), ("d", 1, 0, 0, 1), ("g", 1, 1, 0), ("g", 1, 1, 1),
    ("d", 1, 0, 1, 2), ("d", 1, 1, 0, 1), ("d", 1, 1, 1, 2),
]
```

```python
import jax
import jax.numpy as jnp
from jax import lax
from jax.experimental import pallas as pl
from jax.experimental.pallas import tpu as pltpu
from jax.sharding import PartitionSpec as P

EPS = 1e-05
MIB = 1 << 20
LANES = 128
BUFFERS = 3
DOWN_BUFFERS = 4
VMEM_MIB = 12
PIECES = 8
PARTS = 2
WIDEST = 2048
AXES = ("group", "col", "row", "section")

f32 = jnp.float32
bf16 = jnp.bfloat16


def tile_of(width):
    for tile in (512, 256, 128):
        if width % tile == 0:
            return tile
    return width


def in_vmem(value):
    return pltpu.with_memory_space_constraint(value, pltpu.VMEM)


def in_hbm(value):
    return pltpu.with_memory_space_constraint(value, pltpu.HBM)


VMEM_SPEC = pl.BlockSpec(memory_space=pltpu.VMEM)
HBM_SPEC = pl.BlockSpec(memory_space=pltpu.HBM)
ANY_SPEC = pl.BlockSpec(memory_space=pl.ANY)


class Routes:
    def __init__(self, sizes):
        self.sizes = sizes

    def index(self, place):
        index = 0
        for axis in AXES:
            index = index * self.sizes[axis] + place[axis]
        return index

    def places(self):
        for g in range(self.sizes["group"]):
            for c in range(self.sizes["col"]):
                for r in range(self.sizes["row"]):
                    for s in range(self.sizes["section"]):
                        yield dict(group=g, col=c, row=r, section=s)

    def shifted(self, place, axis, steps):
        return dict(place, **{axis: (place[axis] + steps) % self.sizes[axis]})

    def within(self, section, axis, steps):
        pairs = []
        for place in self.places():
            if place["section"] == section:
                target = self.shifted(place, axis, steps)
            else:
                target = self.shifted(place, "group", 1)
            pairs.append((self.index(place), self.index(target)))
        return pairs

    def onward(self, section, steps):
        pairs = []
        for place in self.places():
            if place["section"] == section:
                target = dict(self.shifted(place, "col", steps), section=section + 1)
            elif place["section"] == section + 1:
                target = dict(place, section=section)
            else:
                target = self.shifted(place, "group", 1)
            pairs.append((self.index(place), self.index(target)))
        return pairs


def streamed(count, parts, slots, copy, body):
    def start(q):
        tile, part = (q // parts, q % parts) if isinstance(q, int) else (lax.div(q, parts), lax.rem(q, parts))
        copy(tile, part, q % slots if isinstance(q, int) else lax.rem(q, slots)).start()

    for q in range(min(slots, count * parts)):
        start(q)

    def step(i, carry):
        def use(part, f):
            q = i * parts + part
            slot = lax.rem(q, slots)
            copy(i, part, slot).wait()
            value = f(slot)

            @pl.when(q + slots < count * parts)
            def _():
                start(q + slots)

            return value

        body(i, use)
        return carry

    return lambda: lax.fori_loop(0, count, step, 0)


class Kernels:
    def __init__(self, n_row, n_col, w_gate, w_up, w_down):
        self.n_row, self.n_col = n_row, n_col
        self.w_up, self.w_down = w_up, w_down
        self.kept = []
        self.before = []
        self.share = 1
        self.depth, self.width = w_gate.shape[1:]
        self.half = self.depth // PARTS
        self.w_gate = w_gate

    def call(self, section, kernel, operands, specs, out_shape, scratch, vmem, flops, moved, name):
        extras = [in_vmem(v) for v in self.kept] + self.before
        n_kept, n = len(self.kept), len(extras)

        def wrapped(*refs):
            if section is None:
                kernel(refs[:n_kept], *refs[n:])
            else:

                @pl.when(lax.axis_index("section") == section)
                def _():
                    kernel(refs[:n_kept], *refs[n:])

        outs = pl.pallas_call(
            wrapped,
            out_shape=out_shape,
            in_specs=[VMEM_SPEC] * n_kept + [ANY_SPEC] * (n - n_kept) + specs,
            out_specs=[VMEM_SPEC] * len(out_shape),
            scratch_shapes=scratch,
            compiler_params=pltpu.CompilerParams(vmem_limit_bytes=vmem * MIB),
            cost_estimate=pl.CostEstimate(flops=flops // self.share, bytes_accessed=moved // self.share, transcendentals=0),
            name=name,
        )(*extras, *operands)
        self.before = [outs[-1]]
        return outs

    def load(self, section):
        self.kept = []
        rows = self.depth // PIECES
        n = PIECES

        def kernel(_, gate_ref, *refs):
            outs, sem = refs[:-1], refs[-1]
            copies = []
            for i, out in enumerate(outs):
                copies.append(pltpu.make_async_copy(gate_ref.at[0, pl.ds(i * rows, rows)], out, sem.at[i]))
            for copy in copies:
                copy.start()
            for copy in copies:
                copy.wait()

        self.kept = self.call(
            section,
            kernel,
            [in_hbm(self.w_gate)],
            [HBM_SPEC],
            [pltpu.VMEM((rows, self.width), bf16)] * n,
            [pltpu.SemaphoreType.DMA((n,))],
            1,
            0,
            2 * n * rows * self.width,
            "load",
        )

    def gate_up(self, section, blocks, scaled_in, gain, start, size, tile):
        depth, half = self.depth, self.half
        opens = scaled_in is None
        n = len(blocks) if opens else 1
        rows = sum(b.shape[0] for b in blocks) if opens else scaled_in.shape[0]
        extra = LANES if opens else 0
        piece = depth // PIECES

        def scale_rows(block_refs, gain_ref, scaled, out):
            tok = block_refs[0].shape[0]
            lane = lax.broadcasted_iota(jnp.int32, (tok, LANES), 1)
            for d, block in enumerate(block_refs):
                place = slice(d * tok, (d + 1) * tok)
                total = jnp.zeros((tok, LANES), f32)
                for first in range(0, depth, tile):
                    wide = block[:, first : first + tile].astype(f32)
                    scaled[place, first : first + tile] = (
                        wide * gain_ref[:, first : first + tile]
                    ).astype(bf16)
                    wide = wide * wide
                    for lane_first in range(0, tile, LANES):
                        total = total + wide[:, lane_first : lane_first + LANES]
                total = jnp.broadcast_to(jnp.sum(total, axis=1, keepdims=True), (tok, LANES))
                high = total.astype(bf16).astype(f32)
                out[place, pl.ds(2 * size, LANES)] = jnp.where(
                    lane < LANES // 2, high, total - high
                ).astype(bf16)

        def kernel(kept, *refs):
            sources, gain_ref, up_w, refs = refs[:n], refs[n], refs[n + 1], refs[n + 2 :]
            out, buf, sem = refs[0], refs[-2], refs[-1]

            def copy(i, part, slot):
                columns = pl.ds(pl.multiple_of(start + i * tile, LANES), tile)
                return pltpu.make_async_copy(
                    up_w.at[0, pl.ds(part * half, half), columns], buf.at[slot], sem.at[slot]
                )

            def body(i, use):
                offset = pl.multiple_of(i * tile, tile)
                columns = pl.ds(pl.multiple_of(start + offset, LANES), tile)

                def product(first, weights):
                    return jnp.dot(
                        scaled[:, first : first + weights.shape[0]], weights, preferred_element_type=f32
                    )

                gate = product(0, kept[0][:, columns])
                for p in range(1, PIECES):
                    gate = gate + product(p * piece, kept[p][:, columns])
                out[:, pl.ds(offset, tile)] = gate.astype(bf16)
                up = use(0, lambda slot: product(0, buf[slot]))
                for part in range(1, PARTS):
                    up = up + use(part, lambda slot: product(part * half, buf[slot]))
                out[:, pl.ds(pl.multiple_of(size + offset, tile), tile)] = up.astype(bf16)

            run = streamed(size // tile, PARTS, BUFFERS, copy, body)
            scaled = sources[0]
            if opens:
                scaled = refs[1]
                scale_rows(sources, gain_ref, scaled, out)
            run()

        out_shape = [pltpu.VMEM((rows, 2 * size + extra), bf16)]
        if opens:
            out_shape += [pltpu.VMEM((rows, depth), bf16)]
        sources = [in_vmem(v) for v in blocks] if opens else [in_vmem(scaled_in)]
        return self.call(
            section,
            kernel,
            sources + [gain, in_hbm(self.w_up)],
            [VMEM_SPEC] * (n + 1) + [HBM_SPEC],
            out_shape,
            [
                pltpu.VMEM((BUFFERS, half, tile), bf16),
                pltpu.SemaphoreType.DMA((BUFFERS,)),
            ],
            VMEM_MIB,
            4 * rows * depth * size,
            2 * depth * size,
            "gate_up",
        )

    def down(self, section, sums, chunks, scale_in, acc):
        n_row, n_col = self.n_row, self.n_col
        start, size = chunks[0][0], sum(chunk[1] for chunk in chunks)
        rows = sums[0][0].shape[0]
        tok = rows // n_col
        columns = self.w_down.shape[2]
        tile = tile_of(columns)
        opens, last = start == 0, start + size == self.width
        parts = -(-size // WIDEST)
        deep = size // parts
        slots = DOWN_BUFFERS
        features = self.depth * n_row
        flat = [in_vmem(v) for group in sums for v in group]
        n = len(flat)

        def kernel(_, *refs):
            sum_refs, w_ref, refs = refs[:n], refs[n], refs[n + 1 :]
            if not opens:
                scale_ref, acc_ref, refs = refs[0], refs[1], refs[2:]
            outs, (held, buf, sem) = refs[:-3], refs[-3:]

            def copy(i, part, slot):
                place = pl.ds(pl.multiple_of(i * tile, tile), tile)
                return pltpu.make_async_copy(
                    w_ref.at[0, pl.ds(start + part * deep, deep), place], buf.at[slot], sem.at[slot]
                )

            def body(i, use):
                place = pl.ds(pl.multiple_of(i * tile, tile), tile)
                total = None if opens else acc_ref[:, place]
                for p in range(parts):
                    left = held[:, p * deep : (p + 1) * deep]
                    part = use(p, lambda slot: jnp.dot(left, buf[slot], preferred_element_type=f32))
                    total = part if total is None else total + part
                if last:
                    total = total.astype(bf16)
                    for d, out in enumerate(outs):
                        out[:, place] = total[d * tok : (d + 1) * tok]
                else:
                    outs[0][:, place] = total

            run = streamed(columns // tile, parts, slots, copy, body)
            for first in range(0, rows, tok):
                place = slice(first, first + tok)
                for c, (begin, width) in enumerate(chunks):
                    refs_here = sum_refs[c * n_row : (c + 1) * n_row]

                    def whole(columns):
                        total = refs_here[0][place, columns].astype(f32)
                        for ref in refs_here[1:]:
                            total = total + ref[place, columns].astype(f32)
                        return total

                    if c == 0 and opens:
                        squares = whole(pl.ds(2 * width, LANES))
                        squares = squares[:, 0:1] + squares[:, LANES // 2 : LANES // 2 + 1]
                        scale = lax.rsqrt(squares / features + EPS)
                    elif c == 0:
                        scale = scale_ref[place, 0:1]
                    step = tile_of(width)
                    for at in range(0, width, step):
                        gate = whole(pl.ds(at, step)) * scale
                        up = whole(pl.ds(width + at, step)) * scale
                        held[place, begin - start + at : begin - start + at + step] = (
                            gate / (1.0 + jnp.exp(-gate)) * up
                        ).astype(bf16)
                if not last:
                    outs[1][place, :] = jnp.broadcast_to(scale, (tok, LANES))
            run()

        if last:
            out_shape = [pltpu.VMEM((tok, columns), bf16)] * n_col
        else:
            out_shape = [pltpu.VMEM((rows, columns), f32), pltpu.VMEM((rows, LANES), f32)]
        extras = [] if opens else [in_vmem(scale_in), in_vmem(acc)]
        return self.call(
            section,
            kernel,
            flat + [in_hbm(self.w_down)] + extras,
            [VMEM_SPEC] * n + [HBM_SPEC] + [VMEM_SPEC] * len(extras),
            out_shape,
            [
                pltpu.VMEM((rows, size), bf16),
                pltpu.VMEM((slots, deep, tile), bf16),
                pltpu.SemaphoreType.DMA((slots,)),
            ],
            VMEM_MIB,
            2 * rows * size * columns,
            2 * size * columns,
            "down",
        )


def solution(mesh):
    sizes = dict(mesh.shape)
    routes = Routes(sizes)
    n_col, n_row, n_section = sizes["col"], sizes["row"], sizes["section"]

    def move(value, pairs):
        return lax.ppermute(value, AXES, pairs)

    def on_device(tokens, norm_gain, w_gate, w_up, w_down):
        section_index = lax.axis_index("section")
        micro, tok, depth = tokens.shape
        width = w_gate.shape[2]
        tile = tile_of(width)
        k = Kernels(n_row, n_col, w_gate, w_up, w_down)

        def gathered(section, block):
            return [block] + [move(block, routes.within(section, "col", d)) for d in range(1, n_col)]

        def exchanged(section, value):
            return [value] + [move(value, routes.within(section, "row", e)) for e in range(1, n_row)]

        class Job:
            def __init__(self, section, block, chunks):
                self.section, self.chunks = section, chunks
                self.blocks = gathered(section, block)
                self.scaled = self.scale = self.acc = None
                self.sums = []

            def gate_up(self, c):
                outs = k.gate_up(self.section, self.blocks, self.scaled, norm_gain, *self.chunks[c], tile)
                if c == 0:
                    self.scaled = outs[1]
                self.sums.append(exchanged(self.section, outs[0]))

            def down(self, first, last):
                outs = k.down(
                    self.section, self.sums[first:last], self.chunks[first:last], self.scale, self.acc
                )
                if last < len(self.chunks):
                    self.acc, self.scale = outs
                    return
                block = self.blocks[0]
                if self.section + 1 < n_section:
                    arrived = [move(outs[d], routes.onward(self.section, -d)) for d in range(n_col)]
                    if self.section:
                        block = move(block, routes.onward(self.section, 0))
                else:
                    arrived = [outs[0]] + [
                        move(outs[d], routes.within(self.section, "col", -d)) for d in range(1, n_col)
                    ]
                total = block.astype(f32)
                for value in arrived:
                    total = total + value.astype(f32)
                self.result = total.astype(bf16)

        jobs = {}
        steps = FLAT if (n_section, micro) == (2, 2) else in_turn(n_section, micro)
        for at, (what, section, m, *c) in enumerate(steps):
            k.share = SHARES.get((what, section, m, *c), 1)
            if what == "n":
                block = jobs[section - 1, m].result if section else tokens[m]
                if k.before and jobs:
                    block, _ = lax.optimization_barrier((block, k.before[0]))
                jobs[section, m] = Job(section, block, chunked(width, tile, *c))
            elif what == "l":
                k.load(section)
            elif what == "g":
                jobs[section, m].gate_up(*c)
                later = [step[0] for step in steps[at + 1 :] if step[0] in "gl"]
                if later[:1] != ["g"]:
                    k.kept = []
            else:
                jobs[section, m].down(*c)
        outs = [
            jnp.stack([jobs[section, m].result for m in range(micro)], axis=0)
            for section in range(n_section)
        ]
        outs = [move(v, routes.onward(s, 0)) for s, v in enumerate(outs[:-1])] + outs[-1:]
        out = outs[0]
        for section in range(1, n_section):
            out = jnp.where(section_index == section, outs[section], out)
        return out[None]

    placed = (
        P(None, ("group", "col"), "row"),
        P("section", "row"),
        P("section", "row", "col"),
        P("section", "row", "col"),
        P("section", "col", "row"),
    )
    return jax.shard_map(
        on_device,
        mesh=mesh,
        in_specs=placed,
        out_specs=P("section", None, ("group", "col"), "row"),
        check_vma=False,
    )


def chunked(width, tile, count):
    tiles = width // tile
    chunks, start = [], 0
    for c in range(count):
        size = -(-(tiles - start // tile) // (count - c)) * tile
        chunks.append((start, size))
        start += size
    return chunks


def in_turn(n_section, micro):
    steps = []
    for section in range(n_section):
        steps += [("l", section, 0)]
        for m in range(micro):
            steps += [("n", section, m, 2), ("g", section, m, 0), ("g", section, m, 1)]
            steps += [("d", section, m, 0, 2)]
    return steps


SHARES = {("g", 1, 0, 0): 3, ("g", 1, 0, 1): 3, ("d", 1, 1, 0, 1): 10, ("d", 1, 1, 1, 2): 10}

FLAT = [
    ("l", None, 0),
    ("n", 0, 0, 2), ("g", 0, 0, 0), ("n", 0, 1, 2), ("g", 0, 0, 1), ("g", 0, 1, 0), ("d", 0, 0, 0, 1),
    ("d", 0, 0, 1, 2), ("g", 0, 1, 1), ("d", 0, 1, 0, 1), ("n", 1, 0, 2), ("d", 0, 1, 1, 2),
    ("g", 1, 0, 0), ("g", 1, 0, 1), ("n", 1, 1, 2), ("d", 1, 0, 0, 1), ("g", 1, 1, 0), ("g", 1, 1, 1),
    ("d", 1, 0, 1, 2), ("d", 1, 1, 0, 1), ("d", 1, 1, 1, 2),
]
```
